128 devices in a mesh: pair: 32 (over x, y, core), orb: 4 (over z).
Axes of the slice: x: 4, y: 4, z: 4, core: 2. Of those that a mesh axis runs over, the one named last changes fastest.
Arguments:
- integral_tiles: bfloat16 [1536, 40, 128, 128], P(('pair', 'orb')), may hold values from -6 to 6
- tile_lam: int32 [1536], P(('pair', 'orb')), may hold values from 0 to 95
- tile_sig: int32 [1536], P(('pair', 'orb')), may hold values from 0 to 2
- tile_rows: int32 [1536], P(('pair', 'orb')), may hold values from 1 to 40
- screen_mask: int32 [1536], P(('pair', 'orb')), may hold values 0 or 1
- occ_panel: bfloat16 [64, 12288], P(None, ('pair', 'orb')), may hold values from -0.5 to 0.5
- virt_panel: bfloat16 [12288, 11264], P('pair', 'orb'), may hold values from -0.0546875 to 0.0546875
Outputs:
- transformed: bfloat16 [64, 40, 11264], P('pair', None, 'orb')
The draws below stay inside these ranges and needn't reach their ends.
All inputs are finite; a program needn't handle non-finite values. No bound on the sum of `screen_mask` on one device may be relied on, other than what follows from the above.
Results may differ from the reference program's by a relative error of at most 0.033.
Values may be sent and summed in bfloat16 or wider, within the bound.
A program may use at most 128 MiB of HBM per device.

```python
import jax
import jax.numpy as jnp
from jax import lax

BS = 128
NBLK = 96
NAO = 12288
NOCC = 64
NV = 11264
R = 40
TILE_DEV = 12
TILES = 1536
BPD = 3
N_PAIR = 32
N_ORB = 4


def touch_ends(array, own_key, low, top_value):
    index_at = [jax.random.randint(jax.random.fold_in(own_key, axis), (), 0, length) for axis, length in enumerate(array.shape)]
    widest = array.shape.index(max(array.shape))
    neighbour = index_at[:widest] + [(index_at[widest] + 1) % array.shape[widest]] + index_at[widest + 1:]
    return array.at[tuple(index_at)].set(low).at[tuple(neighbour)].set(top_value)


def levels(rng, dims, cuts, least, top_value):
    gain, own = 1.0, jax.random.fold_in(rng, 6)
    for position, shards_of in cuts:
        heights = jnp.exp(jax.random.uniform(jax.random.fold_in(own, position), (shards_of,), jnp.float32, least / len(cuts), top_value / len(cuts)))
        gain = gain * jnp.repeat(heights, dims[position] // shards_of).reshape([-1 if axis == position else 1 for axis in range(len(dims))])
    return gain


def bell_draw(stream_key, shape, width, most, shards=(), kind=jnp.bfloat16):
    values = width * jax.random.normal(stream_key, shape, jnp.float32)
    if shards:
        values = values * levels(stream_key, shape, shards, -0.22, 0.18)
    return jnp.clip(values, -most, most).astype(kind)


def setup_inputs(seed: int = 0) -> dict:
    key_list = jax.random.split(jax.random.key(seed), 8)
    return {
        "integral_tiles": bell_draw(key_list[0], (TILES, R, BS, BS), 1.0, 6.0, ((0, 128),)),
        "tile_lam": touch_ends(jax.random.randint(key_list[1], (TILES,), 0, NBLK), jax.random.fold_in(key_list[1], 1), 0, NBLK - 1).astype(jnp.int32),
        "tile_sig": touch_ends(jax.random.randint(key_list[2], (TILES,), 0, BPD), jax.random.fold_in(key_list[2], 1), 0, BPD - 1).astype(jnp.int32),
        "tile_rows": touch_ends(jax.random.randint(key_list[3], (TILES,), 1, R + 1), jax.random.fold_in(key_list[3], 1), 1, R).astype(jnp.int32),
        "screen_mask": touch_ends((jax.random.randint(key_list[4], (TILES,), 0, 3) < 2).astype(jnp.int32), jax.random.fold_in(key_list[4], 1), 0, 1),
        "occ_panel": bell_draw(key_list[5], (NOCC, NAO), BS ** -0.5, 0.5, ((1, 128),)),
        "virt_panel": bell_draw(key_list[6], (NAO, NV), NAO ** -0.5, 0.0546875, ((0, 32), (1, 4))),
    }


def reference(integral_tiles, tile_lam, tile_sig, tile_rows, screen_mask, occ_panel, virt_panel):
    occ_blocks = occ_panel.reshape(NOCC, NBLK, BS)
    row_ids = jnp.arange(R, dtype=jnp.int32)

    def add_tile(totals, items):
        tile, lam_block, sig_local, rows_kept, screened, slot_index = items
        owner = slot_index // (TILE_DEV * N_ORB)
        sig_block = (owner * BPD + sig_local).astype(jnp.int32)
        coeffs = lax.dynamic_index_in_dim(occ_blocks, lam_block.astype(jnp.int32), 1, keepdims=False)
        half_terms = jnp.einsum("jl,rls->jrs", coeffs.astype(jnp.float32), tile.astype(jnp.float32))
        row_live = (row_ids < rows_kept).astype(jnp.float32) * screened.astype(jnp.float32)
        half_terms = half_terms * row_live[None, :, None]
        current = lax.dynamic_index_in_dim(totals, sig_block, 2, keepdims=False)
        totals = lax.dynamic_update_index_in_dim(totals, current + half_terms, sig_block, 2)
        return totals, None

    start_totals = jnp.zeros((NOCC, R, NBLK, BS), jnp.float32)
    slots = jnp.arange(TILES, dtype=jnp.int32)
    totals, _ = lax.scan(add_tile, start_totals, (integral_tiles, tile_lam, tile_sig, tile_rows, screen_mask, slots))
    occ_half = totals.reshape(NOCC * R, N_PAIR, NAO // N_PAIR).astype(jnp.bfloat16)
    virt_ranges = virt_panel.reshape(N_PAIR, NAO // N_PAIR, NV)

    def add_range(result_sum, index):
        left = lax.dynamic_index_in_dim(occ_half, index, 1, keepdims=False)
        right = lax.dynamic_index_in_dim(virt_ranges, index, 0, keepdims=False)
        partial_sum = jnp.dot(left, right, preferred_element_type=jnp.float32).astype(jnp.bfloat16)
        partial_sum = lax.optimization_barrier(partial_sum)
        return result_sum + partial_sum.astype(jnp.float32), None

    result_sum, _ = lax.scan(add_range, jnp.zeros((NOCC * R, NV), jnp.float32), jnp.arange(N_PAIR, dtype=jnp.int32))
    return result_sum.reshape(NOCC, R, NV).astype(jnp.bfloat16)
```

```python
import jax
import jax.numpy as jnp
from jax import lax
from jax.experimental import pallas as pl
from jax.experimental.pallas import tpu as pltpu
from jax.sharding import PartitionSpec as P

BS = 128
NOCC = 64
ROWS = 40
SLOTS = 12
NBLK = 96
SIG = 3
KW = 384
NW = 2816
HW = NW // 2
CUT = 768
BR = 80
MESH = pl.DeviceIdType.MESH
F32 = jnp.float32
BF16 = jnp.bfloat16


def place():
    pair = lax.axis_index("pair")
    return pair, pair // 8, (pair // 2) % 4, pair % 2, lax.axis_index("orb")


def pair_of(x, y, c):
    return (x * 4 + y) * 2 + c


def push(src, dst, send_sem, recv_sem, pair, z):
    return pltpu.make_async_remote_copy(
        src_ref=src,
        dst_ref=dst,
        send_sem=send_sem,
        recv_sem=recv_sem,
        device_id=(pair, z),
        device_id_type=MESH,
    )


def gather_kernel(occ_ref, out_ref, zbuf, gat, zs, zr, ss, sr, cs, cr, out_sem):
    pair, x, y, c, z = place()
    barrier = pltpu.get_barrier_semaphore()

    def hello(pair_id, z_id):
        pl.semaphore_signal(barrier, inc=1, device_id=(pair_id, z_id), device_id_type=MESH)

    hello(pair_of(x, y, 1 - c), z)
    for d in range(1, 4):
        hello(pair_of((x + d) % 4, y, c), z)
        hello(pair_of(x, (y + d) % 4, c), z)
        hello(pair, (z + d) % 4)
    zbuf[z] = jnp.concatenate([occ_ref[...], jnp.zeros((NOCC, 32), BF16)], axis=1)
    pl.semaphore_wait(barrier, 10)

    sends = []

    def start(copy):
        copy.start()
        sends.append(copy)
        return copy

    steps = [
        start(push(zbuf.at[z], zbuf.at[z], zs.at[d - 1], zr.at[d - 1], pair, (z + d) % 4))
        for d in range(1, 4)
    ]
    for copy in steps:
        copy.wait_recv()
    whole = jnp.concatenate([zbuf[i][:, :96] for i in range(4)], axis=1)
    for k in range(3):
        gat[x, y, c, k] = whole[:, k * BS : (k + 1) * BS]

    lo, hi = pl.ds(0, 32), pl.ds(32, 32)
    first_a, first_b = [], []
    for d in range(1, 4):
        view = gat.at[x, y, c, :, lo]
        first_a.append(
            start(push(view, view, ss.at[0, d - 1], sr.at[0, d - 1], pair_of((x + d) % 4, y, c), z))
        )
        view = gat.at[x, y, c, :, hi]
        first_b.append(
            start(push(view, view, ss.at[1, d - 1], sr.at[1, d - 1], pair_of(x, (y + d) % 4, c), z))
        )
    other = pair_of(x, y, 1 - c)
    for copy in first_a:
        copy.wait_recv()
    second_a, second_b, across = [], [], []
    row = gat.at[:, y, c, :, lo]
    for d in range(1, 4):
        second_a.append(
            start(push(row, row, ss.at[2, d - 1], sr.at[2, d - 1], pair_of(x, (y + d) % 4, c), z))
        )
    across.append(start(push(row, row, cs.at[0, 0], cr.at[0, 0], other, z)))
    for copy in first_b:
        copy.wait_recv()
    col = gat.at[x, :, c, :, hi]
    for d in range(1, 4):
        second_b.append(
            start(push(col, col, ss.at[3, d - 1], sr.at[3, d - 1], pair_of((x + d) % 4, y, c), z))
        )
    across.append(start(push(col, col, cs.at[1, 0], cr.at[1, 0], other, z)))
    for d in range(1, 4):
        second_a[d - 1].wait_recv()
        row = gat.at[:, (y - d + 4) % 4, c, :, lo]
        across.append(start(push(row, row, cs.at[0, d], cr.at[0, d], other, z)))
        second_b[d - 1].wait_recv()
        col = gat.at[(x - d + 4) % 4, :, c, :, hi]
        across.append(start(push(col, col, cs.at[1, d], cr.at[1, d], other, z)))
    for copy in across:
        copy.wait_recv()
    done = pltpu.make_async_copy(gat, out_ref, out_sem)
    done.start()
    for copy in sends:
        copy.wait_send()
    done.wait()


def gather_panel(occ_panel):
    sem = pltpu.SemaphoreType.DMA
    return pl.pallas_call(
        gather_kernel,
        out_shape=jax.ShapeDtypeStruct((4, 4, 2, 3, NOCC, BS), BF16),
        in_specs=[pl.BlockSpec(memory_space=pltpu.VMEM)],
        out_specs=pl.BlockSpec(memory_space=pl.ANY),
        scratch_shapes=[
            pltpu.VMEM((4, NOCC, BS), BF16),
            pltpu.VMEM((4, 4, 2, 3, NOCC, BS), BF16),
            sem((3,)),
            sem((3,)),
            sem((4, 3)),
            sem((4, 3)),
            sem((2, 4)),
            sem((2, 4)),
            sem,
        ],
        compiler_params=pltpu.CompilerParams(
            collective_id=0, has_side_effects=True, vmem_limit_bytes=16 * 2**20
        ),
        name="gather_panel",
    )(occ_panel)


def tiles_kernel(lam, sig, rows, mask, tile_ref, occ_ref, out_ref, lhs, acc):
    step = pl.program_id(0)

    @pl.when(step == 0)
    def _():
        lhs[...] = jnp.zeros_like(lhs)
        for t in range(SLOTS):

            @pl.when(mask[t] > 0)
            def _():
                at = pl.multiple_of(sig[t] * NOCC, NOCC)
                lhs[pl.ds(at, NOCC), t * BS : (t + 1) * BS] = occ_ref[lam[t]]

    left = lhs[...]
    for q in range(4):
        parts = []
        for t in range(SLOTS):
            both = []
            for i in range(2):
                live = step * 8 + 2 * q + i < rows[t]
                tile = tile_ref[t, 2 * q + i]
                both.append(jnp.where(live, tile, jnp.zeros_like(tile)))
            parts.append(jnp.concatenate(both, axis=1))
        got = jnp.dot(left, jnp.concatenate(parts, axis=0), preferred_element_type=F32)
        for i in range(2):
            for s in range(SIG):
                acc[s, pl.ds(step * 8 + 2 * q + i, NOCC, stride=ROWS), :] = got[
                    s * NOCC : (s + 1) * NOCC, i * BS : (i + 1) * BS
                ]

    @pl.when(step == pl.num_programs(0) - 1)
    def _():
        @pl.loop(0, NOCC * ROWS, step=64)
        def _(r):
            r = pl.multiple_of(r, 64)
            for s in range(SIG):
                out_ref[pl.ds(r, 64), s * BS : (s + 1) * BS] = acc[s, pl.ds(r, 64), :].astype(BF16)


def tile_sums(lam, sig, rows, mask, tiles, occ):
    return pl.pallas_call(
        tiles_kernel,
        grid_spec=pltpu.PrefetchScalarGridSpec(
            num_scalar_prefetch=4,
            grid=(ROWS // 8,),
            in_specs=[
                pl.BlockSpec((SLOTS, 8, BS, BS), lambda i, *_: (0, i, 0, 0)),
                pl.BlockSpec((NBLK, NOCC, BS), lambda i, *_: (0, 0, 0)),
            ],
            out_specs=pl.BlockSpec((NOCC * ROWS, KW), lambda i, *_: (0, 0)),
            scratch_shapes=[
                pltpu.VMEM((SIG * NOCC, SLOTS * BS), BF16),
                pltpu.VMEM((SIG, NOCC * ROWS, BS), F32),
            ],
        ),
        out_shape=jax.ShapeDtypeStruct((NOCC * ROWS, KW), BF16),
        compiler_params=pltpu.CompilerParams(vmem_limit_bytes=48 * 2**20),
        name="tile_sums",
    )(lam, sig, rows, mask, tiles, occ)


CHUNKS = [
    [(2, 2), (2, 1), (2, 3), (2, 0)],
    [(1, 2), (3, 2), (1, 0), (3, 0)],
    [(1, 1), (1, 3), (3, 1), (3, 3)],
    [(0, 2), (0, 1), (0, 3), (0, 0)],
]
AT = {block: (k, i) for k, chunk in enumerate(CHUNKS) for i, block in enumerate(chunk)}
UP = (2, 1)


def transform_kernel(
    a_ref, b_ref, out_ref, b2, zin, red, a2, cc, ra, rb, rc, rd, re, rf, rg, rh,
    b_sem, zss, zrs, ags, agr, as_, ar, bs_, br, cs_, cr, ds_, dr, es_, er, fs_, fr, gs_, gr, hs_, hr,
):
    pair, x, y, c, z = place()
    barrier = pltpu.get_barrier_semaphore()
    xs = {1: pair_of((x + 1) % 4, y, c), -1: pair_of((x + 3) % 4, y, c)}
    ys = {1: pair_of(x, (y + 1) % 4, c), -1: pair_of(x, (y + 3) % 4, c)}

    def hello(pair_id, z_id):
        pl.semaphore_signal(barrier, inc=1, device_id=(pair_id, z_id), device_id_type=MESH)

    for d in range(4):
        if d:
            hello(pair, (z + d) % 4)
        hello(pair_of(x, y, 1 - c), (z + d) % 4)
    for d in (1, -1):
        hello(xs[d], z)
        hello(ys[d], z)
    pl.semaphore_wait(barrier, 11)

    own_k = pl.ds(pl.multiple_of(c * KW, BS), KW)
    other_k = pl.ds(pl.multiple_of((1 - c) * KW, BS), KW)
    b_own = pltpu.make_async_copy(b_ref, b2.at[own_k], b_sem.at[0])
    b_own.start()
    b_away = push(b_ref, b2.at[own_k], b_sem.at[1], b_sem.at[2], pair_of(x, y, 1 - c), z)
    b_away.start()
    sends = [b_away]

    def start(copy):
        copy.start()
        sends.append(copy)

    def z_copies(k):
        for zt in range(4):
            dx, dy = CHUNKS[k][zt]
            block = ((x + dx) % 4) * 4 + (y + dy) % 4
            yield zt, block, push(a_ref.at[block], zin.at[k, z], zss.at[k, zt], zrs.at[k, z], pair, zt)

    def z_send(k):
        for zt, block, copy in z_copies(k):

            @pl.when(z != zt)
            def _():
                copy.start()

            @pl.when(z == zt)
            def _():
                zin[k, zt] = a_ref[block]

    def z_reduce(k):
        for zf in range(4):

            @pl.when(z != zf)
            def _():
                push(zin.at[k, zf], zin.at[k, zf], zss.at[k, zf], zrs.at[k, zf], pair, zf).wait_recv()

        for core in range(2):
            for r in range(0, BR, 16):
                total = zin[k, 0, core, r : r + 16].astype(F32)
                for zf in range(1, 4):
                    total = total + zin[k, zf, core, r : r + 16].astype(F32)
                red[k, core, r : r + 16] = total.astype(BF16)

    def spread_copies(k):
        for core in range(2):
            for zt in range(4):
                remote = jnp.logical_or(c != core, z != zt)
                yield remote, push(
                    red.at[k, core], a2.at[k, c, z], ags.at[k, core, zt], agr.at[k, c, z],
                    pair_of(x, y, core), zt,
                )

    def spread(k):
        for remote, copy in spread_copies(k):

            @pl.when(remote)
            def _():
                copy.start()

        a2[k, c, z] = red[k, c]

    def spread_wait(k):
        for core in range(2):
            for zf in range(4):

                @pl.when(jnp.logical_or(c != core, z != zf))
                def _():
                    push(
                        red.at[k, core], a2.at[k, core, zf], ags.at[k, core, zf], agr.at[k, core, zf],
                        pair_of(x, y, core), zf,
                    ).wait_recv()

    def multiply(k):
        left = jnp.concatenate([a2[k, i].reshape(4 * BR, KW) for i in range(2)], axis=1)

        def tile(h, at, width):
            got = jnp.dot(left, b2[:, pl.ds(h * HW + at, width)], preferred_element_type=F32)
            cc[k, h, :, :, pl.ds(at, width)] = got.astype(BF16).reshape(4, BR, width)

        for h in range(2):

            @pl.loop(0, HW // 256)
            def _(j):
                tile(h, pl.multiple_of(j * 256, 256), 256)

            tile(h, HW - BS, BS)

    def held(h, block):
        k, i = AT[block]
        return cc.at[k, h, i]

    def add(into, terms, lo=0, hi=HW, out=None):
        for r in range(0, BR, 16):
            total = into[r : r + 16, lo:hi].astype(F32)
            for term in terms:
                total = total + term[r : r + 16, lo:hi].astype(F32)
            if out is None:
                into[r : r + 16, lo:hi] = total.astype(BF16)
            else:
                out_ref[r : r + 16, out : out + hi - lo] = total.astype(BF16)

    halves = {1: pl.ds(0, CUT), -1: pl.ds(CUT, HW - CUT)}

    def halves_out(src, dst, send_sem, recv_sem, to):
        for i, d in enumerate((1, -1)):
            start(push(src.at[:, halves[d]], dst.at[:, halves[d]], send_sem.at[i], recv_sem.at[i], to[d], z))

    def half_add(into, dst, send_sem, recv_sem, d, to):
        i = 0 if d == 1 else 1
        push(dst.at[:, halves[d]], dst.at[:, halves[d]], send_sem.at[i], recv_sem.at[i], to[d], z).wait_recv()
        add(into, [dst], 0 if d == 1 else CUT, CUT if d == 1 else HW)

    def arrived(dst, send_sem, recv_sem):
        push(dst, dst, send_sem, recv_sem, pair_of(x, y, 1 - c), z).wait_recv()

    def x_far():
        for dy in (2, 1, 3, 0):
            d = 1 if dy in UP else -1
            start(push(held(0, (2, dy)), ra.at[dy], as_.at[dy], ar.at[dy], xs[d], z))

    def x_near(blocks):
        order = sorted(blocks, key=lambda b: (b[1] in UP) == (b[0] == 1))
        for dx, dy in order:
            d = 1 if dx == 1 else -1
            if (dy in UP) == (dx == 1):
                arrived(ra.at[dy], as_.at[dy], ar.at[dy])
                add(held(0, (dx, dy)), [ra.at[dy]])
            i = 0 if d == 1 else 1
            start(push(held(0, (dx, dy)), rb.at[i, dy], bs_.at[i, dy], br.at[i, dy], xs[d], z))

    def x_home(dy):
        for i in range(2):
            arrived(rb.at[i, dy], bs_.at[i, dy], br.at[i, dy])
        add(held(0, (0, dy)), [rb.at[0, dy], rb.at[1, dy]])

    def near(h, block, far, far_s, far_r, dst, send_sem, recv_sem, d, to):
        half_add(held(h, block), far, far_s, far_r, d, to)
        i = 0 if d == 1 else 1
        start(push(held(h, block), dst.at[i], send_sem.at[i], recv_sem.at[i], to[d], z))

    def y_far(dx):
        halves_out(held(1, (dx, 2)), re.at[dx], es_.at[dx], er.at[dx], ys)

    def y_near(dx):
        for d in (1, -1):
            near(1, (dx, d % 4), re.at[dx], es_.at[dx], er.at[dx], rf.at[dx], fs_.at[dx], fr.at[dx], d, ys)

    def y_home(dx):
        for i in range(2):
            arrived(rf.at[dx, i], fs_.at[dx, i], fr.at[dx, i])
        add(held(1, (dx, 0)), [rf.at[dx, 0], rf.at[dx, 1]])

    z_send(0)
    z_send(1)
    z_reduce(0)
    spread(0)
    z_send(2)
    z_reduce(1)
    spread(1)
    z_send(3)
    b_own.wait()
    push(b_ref, b2.at[other_k], b_sem.at[1], b_sem.at[2], pair_of(x, y, 1 - c), z).wait_recv()
    spread_wait(0)
    multiply(0)
    y_far(2)
    x_far()
    z_reduce(2)
    spread(2)
    y_near(2)
    spread_wait(1)
    multiply(1)
    y_far(1)
    y_far(3)
    x_near(CHUNKS[1])
    z_reduce(3)
    spread(3)
    spread_wait(2)
    multiply(2)
    y_near(1)
    y_near(3)
    x_near(CHUNKS[2])
    y_home(2)
    halves_out(held(1, (2, 0)), rg, gs_, gr, xs)
    spread_wait(3)
    multiply(3)
    y_far(0)
    x_home(2)
    halves_out(held(0, (0, 2)), rc, cs_, cr, ys)
    y_home(1)
    near(1, (1, 0), rg, gs_, gr, rh, hs_, hr, 1, xs)
    y_home(3)
    near(1, (3, 0), rg, gs_, gr, rh, hs_, hr, -1, xs)
    y_near(0)
    x_home(1)
    near(0, (0, 1), rc, cs_, cr, rd, ds_, dr, 1, ys)
    x_home(3)
    near(0, (0, 3), rc, cs_, cr, rd, ds_, dr, -1, ys)
    x_home(0)
    y_home(0)
    for i in range(2):
        arrived(rh.at[i], hs_.at[i], hr.at[i])
    add(held(1, (0, 0)), [rh.at[0], rh.at[1]], out=HW)
    for i in range(2):
        arrived(rd.at[i], ds_.at[i], dr.at[i])
    add(held(0, (0, 0)), [rd.at[0], rd.at[1]], out=0)

    for copy in sends:
        copy.wait_send()
    for k in range(4):
        for zt, _, copy in z_copies(k):

            @pl.when(z != zt)
            def _():
                copy.wait_send()

        for remote, copy in spread_copies(k):

            @pl.when(remote)
            def _():
                copy.wait_send()


def transform(a, b):
    sem = pltpu.SemaphoreType.DMA

    def vm(*shape):
        return pltpu.VMEM(shape, BF16)

    pairs = [(4,), (2, 4), (2,), (2,), (4, 2), (4, 2), (2,), (2,)]
    return pl.pallas_call(
        transform_kernel,
        out_shape=jax.ShapeDtypeStruct((BR, NW), BF16),
        in_specs=[pl.BlockSpec(memory_space=pltpu.VMEM), pl.BlockSpec(memory_space=pl.ANY)],
        out_specs=pl.BlockSpec(memory_space=pltpu.VMEM),
        scratch_shapes=[
            vm(2 * KW, NW),
            vm(4, 4, 2, BR, KW),
            vm(4, 2, BR, KW),
            vm(4, 2, 4, BR, KW),
            vm(4, 2, 4, BR, HW),
            vm(4, BR, HW),
            vm(2, 4, BR, HW),
            vm(BR, HW),
            vm(2, BR, HW),
            vm(4, BR, HW),
            vm(4, 2, BR, HW),
            vm(BR, HW),
            vm(2, BR, HW),
            sem((3,)),
            sem((4, 4)),
            sem((4, 4)),
            sem((4, 2, 4)),
            sem((4, 2, 4)),
            *[sem(shape) for shape in pairs for _ in range(2)],
        ],
        compiler_params=pltpu.CompilerParams(
            collective_id=1, has_side_effects=True, vmem_limit_bytes=56 * 2**20
        ),
        name="transform",
    )(a, b)


def body(integral_tiles, tile_lam, tile_sig, tile_rows, screen_mask, occ_panel, virt_panel):
    occ = gather_panel(occ_panel).reshape(NBLK, NOCC, BS)
    sums = tile_sums(tile_lam, tile_sig, tile_rows, screen_mask, integral_tiles, occ)
    out = transform(sums.reshape(16, 2, BR, KW), virt_panel)
    return out.reshape(2, ROWS, NW)


def solution(mesh):
    return jax.shard_map(
        body,
        mesh=mesh,
        in_specs=(
            P(("pair", "orb"), None, None, None),
            P(("pair", "orb")),
            P(("pair", "orb")),
            P(("pair", "orb")),
            P(("pair", "orb")),
            P(None, ("pair", "orb")),
            P("pair", "orb"),
        ),
        out_specs=P("pair", None, "orb"),
        check_vma=False,
    )
```

```python
import jax
import jax.numpy as jnp
from jax import lax
from jax.experimental import pallas as pl
from jax.experimental.pallas import tpu as pltpu
from jax.sharding import PartitionSpec as P

BS = 128
NOCC = 64
ROWS = 40
SLOTS = 12
NBLK = 96
SIG = 3
KW = 384
NW = 2816
HW = NW // 2
CUT = 768
BR = 80
MESH = pl.DeviceIdType.MESH
F32 = jnp.float32
BF16 = jnp.bfloat16

CHUNKS = [
    [(2, 2), (2, 1)],
    [(1, 2), (2, 3)],
    [(3, 2), (2, 0)],
    [(0, 2), (1, 1)],
    [(3, 3), (1, 3)],
    [(3, 1), (1, 0)],
    [(3, 0), (0, 1)],
    [(0, 3), (0, 0)],
]
NC = len(CHUNKS)
AT = {block: (k, i) for k, chunk in enumerate(CHUNKS) for i, block in enumerate(chunk)}


def pair_of(x, y, c):
    return (x * 4 + y) * 2 + c


def push(src, dst, send_sem, recv_sem, pair, z):
    return pltpu.make_async_remote_copy(
        src_ref=src,
        dst_ref=dst,
        send_sem=send_sem,
        recv_sem=recv_sem,
        device_id=(pair, z),
        device_id_type=MESH,
    )


def fused_kernel(
    tiles_hbm, lam_hbm, sig_hbm, rows_hbm, mask_hbm, occ_ref, b_hbm, out_ref,
    tiles, ints, b2, zbuf, gat, lhs, acc, a, zra, zrb, red, a2, cc, r1, r2, r3, r4,
    in_sem, b_sem, gz_s, gz_r, ga_s, ga_r, gc_s, gc_r,
    za_s, za_r, zb_s, zb_r, zc_s, zc_r, zd_s, zd_r,
    r1_s, r1_r, r2_s, r2_r, r3_s, r3_r, r4_s, r4_r,
):
    pair = lax.axis_index("pair")
    z = lax.axis_index("orb")
    x, y, c = pair // 8, (pair // 2) % 4, pair % 2
    other = pair_of(x, y, 1 - c)
    up, down = (z + 1) % 4, (z + 3) % 4
    xs = {1: pair_of((x + 1) % 4, y, c), -1: pair_of((x + 3) % 4, y, c)}
    ys = {1: pair_of(x, (y + 1) % 4, c), -1: pair_of(x, (y + 3) % 4, c)}
    first, second = (xs, ys), (ys, xs)

    own_k = pl.ds(pl.multiple_of(c * KW, BS), KW)
    other_k = pl.ds(pl.multiple_of((1 - c) * KW, BS), KW)
    b_own = pltpu.make_async_copy(b_hbm, b2.at[own_k], b_sem.at[0])
    b_own.start()
    locals_ = []
    for i, ref in enumerate((lam_hbm, sig_hbm, rows_hbm, mask_hbm)):
        locals_.append(pltpu.make_async_copy(ref, ints.at[i], in_sem.at[i]))
    for i in range(4):
        part = pl.ds(3 * i, 3)
        locals_.append(pltpu.make_async_copy(tiles_hbm.at[part], tiles.at[part], in_sem.at[4 + i]))
    for copy in locals_:
        copy.start()

    barrier = pltpu.get_barrier_semaphore()

    def hello(pair_id, z_id):
        pl.semaphore_signal(barrier, inc=1, device_id=(pair_id, z_id), device_id_type=MESH)

    hello(other, z)
    hello(other, up)
    hello(other, down)
    for d in range(1, 4):
        hello(pair_of((x + d) % 4, y, c), z)
        hello(pair_of(x, (y + d) % 4, c), z)
        hello(pair, (z + d) % 4)
    zbuf[z] = jnp.concatenate([occ_ref[...], jnp.zeros((NOCC, 32), BF16)], axis=1)
    lhs[...] = jnp.zeros_like(lhs)
    pl.semaphore_wait(barrier, 12)

    sends = []

    def start(copy):
        copy.start()
        sends.append(copy)
        return copy

    steps = [
        start(push(zbuf.at[z], zbuf.at[z], gz_s.at[d - 1], gz_r.at[d - 1], pair, (z + d) % 4))
        for d in range(1, 4)
    ]
    b_own.wait()
    b_away = start(push(b2.at[own_k], b2.at[own_k], b_sem.at[1], b_sem.at[2], other, z))
    for copy in steps:
        copy.wait_recv()
    whole = jnp.concatenate([zbuf[i][:, :96] for i in range(4)], axis=1)
    for k in range(3):
        gat[x, y, c, k] = whole[:, k * BS : (k + 1) * BS]
    lo, hi = pl.ds(0, 32), pl.ds(32, 32)
    first_a, first_b = [], []
    for d in range(1, 4):
        view = gat.at[x, y, c, :, lo]
        first_a.append(
            start(push(view, view, ga_s.at[0, d - 1], ga_r.at[0, d - 1], pair_of((x + d) % 4, y, c), z))
        )
        view = gat.at[x, y, c, :, hi]
        first_b.append(
            start(push(view, view, ga_s.at[1, d - 1], ga_r.at[1, d - 1], pair_of(x, (y + d) % 4, c), z))
        )
    for copy in first_a:
        copy.wait_recv()
    second_a, second_b, across = [], [], []
    row = gat.at[:, y, c, :, lo]
    for d in range(1, 4):
        second_a.append(
            start(push(row, row, ga_s.at[2, d - 1], ga_r.at[2, d - 1], pair_of(x, (y + d) % 4, c), z))
        )
    across.append(start(push(row, row, gc_s.at[0, 0], gc_r.at[0, 0], other, z)))
    for copy in first_b:
        copy.wait_recv()
    col = gat.at[x, :, c, :, hi]
    for d in range(1, 4):
        second_b.append(
            start(push(col, col, ga_s.at[3, d - 1], ga_r.at[3, d - 1], pair_of((x + d) % 4, y, c), z))
        )
    across.append(start(push(col, col, gc_s.at[1, 0], gc_r.at[1, 0], other, z)))
    for d in range(1, 4):
        second_a[d - 1].wait_recv()
        row = gat.at[:, (y - d + 4) % 4, c, :, lo]
        across.append(start(push(row, row, gc_s.at[0, d], gc_r.at[0, d], other, z)))
        second_b[d - 1].wait_recv()
        col = gat.at[(x - d + 4) % 4, :, c, :, hi]
        across.append(start(push(col, col, gc_s.at[1, d], gc_r.at[1, d], other, z)))
    for copy in across:
        copy.wait_recv()
    for copy in locals_:
        copy.wait()

    for t in range(SLOTS):
        lam = ints[0, t]
        picked = gat[lam // 24, (lam // 6) % 4, (lam // 3) % 2, lam % 3]
        for s in range(SIG):
            keep = jnp.logical_and(ints[1, t] == s, ints[3, t] > 0)
            lhs[s * NOCC : (s + 1) * NOCC, t * BS : (t + 1) * BS] = jnp.where(
                keep, picked, jnp.zeros_like(picked)
            )

    @pl.loop(0, ROWS // 2, unroll=4)
    def _(q):
        parts = []
        for t in range(SLOTS):
            both = []
            for i in range(2):
                tile = tiles[t, 2 * q + i]
                both.append(jnp.where(2 * q + i < ints[2, t], tile, jnp.zeros_like(tile)))
            parts.append(jnp.concatenate(both, axis=1))
        got = jnp.dot(lhs[...], jnp.concatenate(parts, axis=0), preferred_element_type=F32)
        for i in range(2):
            for s in range(SIG):
                acc[s, pl.ds(2 * q + i, NOCC, stride=ROWS), :] = got[
                    s * NOCC : (s + 1) * NOCC, i * BS : (i + 1) * BS
                ]

    def z_load(k):
        for i, (dx, dy) in enumerate(CHUNKS[k]):
            for core in range(2):
                at = pl.multiple_of(pair_of((x + dx) % 4, (y + dy) % 4, core) * BR, 16)
                for s in range(SIG):
                    a[k, 2 * i + core, :, s * BS : (s + 1) * BS] = acc[s, pl.ds(at, BR), :].astype(BF16)

    def cut(k, d):
        return (0, 48 - 16 * (k % 2)) if d == 1 else (48 - 16 * (k % 2), BR)

    def far_copy(k, d):
        lo, hi = cut(k, d)
        i = 0 if d == 1 else 1
        span = pl.ds(lo, hi - lo)
        return push(
            a.at[k, (z + 2) % 4, span], zra.at[k, span], za_s.at[k, i], za_r.at[k, i], pair, (z + d) % 4
        )

    def near_copy(k, d):
        i = 0 if d == 1 else 1
        return push(a.at[k, (z + d) % 4], zrb.at[k, i], zb_s.at[k, i], zb_r.at[k, i], pair, (z + d) % 4)

    def z_far(k):
        z_load(k)
        for d in (1, -1):
            start(far_copy(k, d))

    def z_near(k):
        for d in (1, -1):
            far_copy(k, d).wait_recv()
            unit = (z + d) % 4
            for r in range(*cut(k, d), 16):
                a[k, unit, r : r + 16] = (
                    a[k, unit, r : r + 16].astype(F32) + zra[k, r : r + 16].astype(F32)
                ).astype(BF16)
            start(near_copy(k, d))

    mine = z % 2 == c

    def out_copy(k, i):
        target, zt = ((other, z), (jnp.where(mine, pair, other), up), (jnp.where(mine, pair, other), down))[i]
        return push(red.at[k], a2.at[k, c, z // 2], zc_s.at[k, i], zc_r.at[k, c, i], target, zt)

    def z_sum(k):
        for d in (1, -1):
            near_copy(k, d).wait_recv()
        for r in range(0, BR, 16):
            red[k, r : r + 16] = (
                a[k, z, r : r + 16].astype(F32)
                + zrb[k, 0, r : r + 16].astype(F32)
                + zrb[k, 1, r : r + 16].astype(F32)
            ).astype(BF16)
        start(out_copy(k, 1))
        start(out_copy(k, 2))

        @pl.when(mine)
        def _():
            a2[k, c, z // 2] = red[k]

        @pl.when(jnp.logical_not(mine))
        def _():
            out_copy(k, 0).start()

    def landed(k, core, zf, i):
        view = a2.at[k, core, zf // 2]
        return push(view, view, zc_s.at[k, i], zc_r.at[k, core, i], other, z)

    def on_copy(k, core):
        zf, zt = (down, up) if core == 0 else (up, down)
        view = a2.at[k, core, zf // 2]
        return push(view, view, zd_s.at[k, core], zd_r.at[k, core], pair, zt)

    def z_on(k):
        @pl.when(jnp.logical_not(mine))
        def _():
            for core, zf, i in ((0, down, 1), (1, up, 2)):
                landed(k, core, zf, i).wait_recv()
                on_copy(k, core).start()

    def z_end(k):
        @pl.when(mine)
        def _():
            landed(k, 1 - c, z, 0).wait_recv()
            for core in range(2):
                view = a2.at[k, core, ((z + 2) % 4) // 2]
                push(view, view, zd_s.at[k, core], zd_r.at[k, core], other, z).wait_recv()

        @pl.when(jnp.logical_not(mine))
        def _():
            landed(k, 1, down, 1).wait_recv()
            landed(k, 0, up, 2).wait_recv()

    def multiply(k):
        left = jnp.concatenate([a2[k, i].reshape(2 * BR, KW) for i in range(2)], axis=1)
        for h in range(2):
            for at in range(0, HW, 512):
                width = min(512, HW - at)
                got = jnp.dot(
                    left, b2[:, h * HW + at : h * HW + at + width], preferred_element_type=F32
                )
                cc[k, h, :, :, at : at + width] = got.astype(BF16).reshape(2, BR, width)

    def held(h, f, s):
        k, i = AT[(f, s) if h == 0 else (s, f)]
        return cc.at[k, h, i]

    def add(into, terms, lo=0, hi=HW, out=None):
        for r in range(0, BR, 16):
            total = into[r : r + 16, lo:hi].astype(F32)
            for term in terms:
                total = total + term[r : r + 16, lo:hi].astype(F32)
            if out is None:
                into[r : r + 16, lo:hi] = total.astype(BF16)
            else:
                out_ref[r : r + 16, out : out + hi - lo] = total.astype(BF16)

    def columns(d):
        return pl.ds(0, CUT) if d == 1 else pl.ds(CUT, HW - CUT)

    def far(src, dst, send_sem, recv_sem, to):
        for i, d in enumerate((1, -1)):
            start(push(src.at[:, columns(d)], dst.at[:, columns(d)], send_sem.at[i], recv_sem.at[i], to[d], z))

    def near(block, d, far_dst, far_s, far_r, dst, send_sem, recv_sem, to):
        i = 0 if d == 1 else 1
        view = far_dst.at[:, columns(d)]
        push(view, view, far_s.at[i], far_r.at[i], to[d], z).wait_recv()
        add(block, [far_dst], 0 if d == 1 else CUT, CUT if d == 1 else HW)
        start(push(block, dst.at[i], send_sem.at[i], recv_sem.at[i], to[d], z))

    def arrived(dst, send_sem, recv_sem):
        for i in range(2):
            push(dst.at[i], dst.at[i], send_sem.at[i], recv_sem.at[i], other, z).wait_recv()

    def far1(h, s):
        far(held(h, 2, s), r1.at[h, s], r1_s.at[h, s], r1_r.at[h, s], first[h])

    def near1(h, s, d):
        near(
            held(h, d % 4, s), d, r1.at[h, s], r1_s.at[h, s], r1_r.at[h, s],
            r2.at[h, s], r2_s.at[h, s], r2_r.at[h, s], first[h],
        )

    def home1(h, s):
        arrived(r2.at[h, s], r2_s.at[h, s], r2_r.at[h, s])
        add(held(h, 0, s), [r2.at[h, s, 0], r2.at[h, s, 1]])

    def far2(h):
        far(held(h, 0, 2), r3.at[h], r3_s.at[h], r3_r.at[h], second[h])

    def near2(h, d):
        near(
            held(h, 0, d % 4), d, r3.at[h], r3_s.at[h], r3_r.at[h], r4.at[h], r4_s.at[h], r4_r.at[h], second[h]
        )

    def final(h):
        arrived(r4.at[h], r4_s.at[h], r4_r.at[h])
        add(held(h, 0, 0), [r4.at[h, 0], r4.at[h, 1]], out=h * HW)

    def pair_steps(k):
        if k == 0:
            far1(0, 2)
            far1(1, 2)
            far1(0, 1)
        if k == 1:
            far1(0, 3)
            far1(1, 1)
            near1(1, 2, 1)
            near1(0, 2, 1)
            near1(1, 2, -1)
        if k == 2:
            far1(0, 0)
            far1(1, 3)
            near1(0, 2, -1)
        if k == 3:
            far1(1, 0)
            near1(0, 1, 1)
            near1(1, 1, 1)
            home1(1, 2)
            far2(1)
        if k == 4:
            near1(0, 3, -1)
            near1(1, 3, -1)
            near1(0, 3, 1)
            near1(1, 1, -1)
            home1(0, 2)
            far2(0)
        if k == 5:
            near1(0, 1, -1)
            near1(1, 3, 1)
            near1(0, 0, 1)
        if k == 6:
            near1(0, 0, -1)
            near1(1, 0, 1)
            home1(1, 1)
            near2(1, 1)
        if k == 7:
            near1(1, 0, -1)
            home1(0, 1)
            near2(0, 1)
            home1(1, 3)
            near2(1, -1)
            home1(0, 3)
            near2(0, -1)
            home1(0, 0)
            home1(1, 0)
            final(1)
            final(0)

    z_far(0)
    for t in range(NC + 3):
        if t + 1 < NC:
            z_far(t + 1)
        if t < NC:
            z_near(t)
        if 0 <= t - 1 < NC:
            z_sum(t - 1)
        if 0 <= t - 2 < NC:
            z_on(t - 2)
        if t == 2:
            push(b2.at[other_k], b2.at[other_k], b_sem.at[1], b_sem.at[2], other, z).wait_recv()
        if t >= 3:
            z_end(t - 3)
            multiply(t - 3)
            pair_steps(t - 3)

    for copy in sends:
        copy.wait_send()
    for k in range(NC):

        @pl.when(jnp.logical_not(mine))
        def _():
            out_copy(k, 0).wait_send()
            for core in range(2):
                on_copy(k, core).wait_send()


def fused(tiles, lam, sig, rows, mask, occ, b):
    sem = pltpu.SemaphoreType.DMA

    def vm(*shape):
        return pltpu.VMEM(shape, BF16)

    def twice(*shapes):
        return [sem(shape) for shape in shapes for _ in range(2)]

    hbm = pl.BlockSpec(memory_space=pl.ANY)
    vmem = pl.BlockSpec(memory_space=pltpu.VMEM)
    return pl.pallas_call(
        fused_kernel,
        out_shape=jax.ShapeDtypeStruct((BR, NW), BF16),
        in_specs=[hbm, hbm, hbm, hbm, hbm, vmem, hbm],
        out_specs=vmem,
        scratch_shapes=[
            vm(SLOTS, ROWS, BS, BS),
            pltpu.SMEM((4, SLOTS), jnp.int32),
            vm(2 * KW, NW),
            vm(4, NOCC, BS),
            vm(4, 4, 2, 3, NOCC, BS),
            vm(SIG * NOCC, SLOTS * BS),
            pltpu.VMEM((SIG, NOCC * ROWS, BS), F32),
            vm(NC, 4, BR, KW),
            vm(NC, BR, KW),
            vm(NC, 2, BR, KW),
            vm(NC, BR, KW),
            vm(NC, 2, 2, BR, KW),
            vm(NC, 2, 2, BR, HW),
            vm(2, 4, BR, HW),
            vm(2, 4, 2, BR, HW),
            vm(2, BR, HW),
            vm(2, 2, BR, HW),
            sem((8,)),
            sem((3,)),
            *twice((3,), (4, 3), (2, 4)),
            *twice((NC, 2), (NC, 2)),
            sem((NC, 3)),
            sem((NC, 2, 3)),
            *twice((NC, 2), (2, 4, 2), (2, 4, 2), (2, 2), (2, 2)),
        ],
        compiler_params=pltpu.CompilerParams(
            collective_id=0, has_side_effects=True, vmem_limit_bytes=60 * 2**20
        ),
        name="fused",
    )(tiles, lam, sig, rows, mask, occ, b)


def body(integral_tiles, tile_lam, tile_sig, tile_rows, screen_mask, occ_panel, virt_panel):
    out = fused(
        integral_tiles, tile_lam, tile_sig, tile_rows, screen_mask, occ_panel, virt_panel
    )
    return out.reshape(2, ROWS, NW)


def solution(mesh):
    return jax.shard_map(
        body,
        mesh=mesh,
        in_specs=(
            P(("pair", "orb"), None, None, None),
            P(("pair", "orb")),
            P(("pair", "orb")),
            P(("pair", "orb")),
            P(("pair", "orb")),
            P(None, ("pair", "orb")),
            P("pair", "orb"),
        ),
        out_specs=P("pair", None, "orb"),
        check_vma=False,
    )
```

```python
import jax
import jax.numpy as jnp
from jax import lax
from jax.experimental import pallas as pl
from jax.experimental.pallas import tpu as pltpu
from jax.sharding import PartitionSpec as P

BS = 128
NOCC = 64
ROWS = 40
SLOTS = 12
NBLK = 96
SIG = 3
KW = 384
NW = 2816
HW = NW // 2
CUT = 768
BR = 80
MESH = pl.DeviceIdType.MESH
F32 = jnp.float32
BF16 = jnp.bfloat16

CHUNKS = [
    [[((2, 1), 0, BR)], [((1, 2), 0, BR)]],
    [[((2, 3), 0, BR)], [((3, 2), 0, BR)]],
    [[((1, 1), 0, 48), ((3, 3), 0, 32)], [((2, 2), 0, BR)]],
    [[((1, 3), 0, BR)], [((3, 1), 0, BR)]],
    [[((0, 3), 0, 32), ((3, 0), 0, 48)], [((2, 0), 0, BR)]],
    [[((1, 1), 48, BR), ((3, 3), 32, BR)], [((0, 2), 0, BR)]],
    [[((0, 1), 0, BR)], [((1, 0), 0, BR)]],
    [[((0, 3), 32, BR), ((3, 0), 48, BR)], [((0, 0), 0, BR)]],
]
NC = len(CHUNKS)
DIRECT = 3

ORDER = [
    ("zf", 0), ("zf", 1), ("zf", 2), ("zs", 0), ("zf", 3), ("zs", 1), ("zf", 4), ("zs", 2), ("zf", 5), ("mm", 0),
    ("f1", 0, 1), ("f1", 1, 1), ("zn", 3), ("mm", 1), ("f1", 0, 3), ("f1", 1, 3), ("zn", 4), ("mm", 2),
    ("f1", 0, 2), ("f1", 1, 2), ("zn", 5), ("n1", 0, 1, 1, 0), ("n1", 1, 1, 1, 0), ("zs", 3), ("n1", 0, 3, -1, 0),
    ("n1", 1, 3, -1, 0), ("zs", 4), ("zs", 5), ("n1", 0, 2, -1, 0), ("n1", 1, 2, -1, 0), ("n1", 0, 2, 1, 0),
    ("n1", 1, 2, 1, 0), ("zo", 3), ("zf", 6), ("zo", 4), ("zf", 7), ("zo", 5), ("mm", 3), ("zn", 6),
    ("n1", 0, 1, -1, 0), ("n1", 0, 3, 1, 0), ("n1", 1, 1, -1, 0), ("zn", 7), ("n1", 1, 3, 1, 0), ("mm", 4),
    ("f1", 0, 0), ("mm", 5), ("f1", 1, 0), ("zs", 6), ("n1", 0, 1, 1, 1), ("n1", 0, 3, -1, 1), ("n1", 1, 1, 1, 1),
    ("zs", 7), ("n1", 1, 3, -1, 1), ("h1", 0, 2, 0), ("f2", 0), ("h1", 1, 2, 0), ("f2", 1), ("zo", 6), ("zo", 7),
    ("n1", 0, 0, -1, 0), ("n1", 1, 0, -1, 0), ("mm", 6), ("n1", 0, 0, 1, 0), ("n1", 1, 0, 1, 0), ("mm", 7),
    ("n1", 0, 0, -1, 1), ("n1", 1, 0, -1, 1), ("h1", 0, 1, 0), ("h1", 0, 3, 0), ("h1", 0, 3, 1), ("h1", 1, 1, 0),
    ("h1", 1, 3, 0), ("h1", 1, 3, 1), ("n2", 1, -1, 0), ("n2", 1, -1, 1), ("n2", 0, -1, 0), ("n2", 0, -1, 1),
    ("n2", 1, 1, 0), ("n2", 0, 1, 0), ("h1", 0, 0, 0), ("h1", 1, 0, 0), ("fi", 1), ("fi", 0),
]


def pieces():
    found = {}
    for k, chunk in enumerate(CHUNKS):
        for i, parts in enumerate(chunk):
            at = 0
            for block, lo, hi in parts:
                found.setdefault(block, []).append((k, i, at, lo, hi))
                at += hi - lo
    return found


PIECES = pieces()


def pair_of(x, y, c):
    return (x * 4 + y) * 2 + c


def push(src, dst, send_sem, recv_sem, pair, z):
    return pltpu.make_async_remote_copy(
        src_ref=src,
        dst_ref=dst,
        send_sem=send_sem,
        recv_sem=recv_sem,
        device_id=(pair, z),
        device_id_type=MESH,
    )


def fused_kernel(
    tiles_hbm, lam_hbm, sig_hbm, rows_hbm, mask_hbm, occ_hbm, b_hbm, out_ref,
    tiles, ints, b2, panel, zbuf, gat, lhs, acc, a, zra, zrb, zdx, red, a2, cc, r1, r2, r3, r4,
    in_sem, b_sem, gz_s, gz_r, ga_s, ga_r, gs_s, gs_r, gc_s, gc_r,
    za_s, za_r, zb_s, zb_r, ze_s, ze_r, zc_s, zc_r, zd_s, zd_r,
    r1_s, r1_r, r2_s, r2_r, r3_s, r3_r, r4_s, r4_r,
):
    pair = lax.axis_index("pair")
    z = lax.axis_index("orb")
    x, y, c = pair // 8, (pair // 2) % 4, pair % 2
    other = pair_of(x, y, 1 - c)
    up, down = (z + 1) % 4, (z + 3) % 4
    xs = {1: pair_of((x + 1) % 4, y, c), -1: pair_of((x + 3) % 4, y, c)}
    ys = {1: pair_of(x, (y + 1) % 4, c), -1: pair_of(x, (y + 3) % 4, c)}
    axes1, axes2 = (xs, ys), (ys, xs)

    own_k = pl.ds(pl.multiple_of(c * KW, BS), KW)
    other_k = pl.ds(pl.multiple_of((1 - c) * KW, BS), KW)
    occ_own = pltpu.make_async_copy(occ_hbm, panel, b_sem.at[3])
    occ_own.start()
    b_own = pltpu.make_async_copy(b_hbm, b2.at[own_k], b_sem.at[0])
    locals_ = []
    for i, ref in enumerate((lam_hbm, sig_hbm, rows_hbm, mask_hbm)):
        locals_.append(pltpu.make_async_copy(ref, ints.at[i], in_sem.at[i]))
    for i in range(4):
        part = pl.ds(3 * i, 3)
        locals_.append(pltpu.make_async_copy(tiles_hbm.at[part], tiles.at[part], in_sem.at[4 + i]))
    for copy in locals_:
        copy.start()
    b_own.start()

    barrier = pltpu.get_barrier_semaphore()

    def hello(pair_id, z_id):
        pl.semaphore_signal(barrier, inc=1, device_id=(pair_id, z_id), device_id_type=MESH)

    hello(other, z)
    hello(other, up)
    hello(other, down)
    for d in range(1, 4):
        hello(pair_of((x + d) % 4, y, c), z)
        hello(pair_of(x, (y + d) % 4, c), z)
        hello(pair, (z + d) % 4)
    occ_own.wait()
    zbuf[z] = jnp.concatenate([panel[...], jnp.zeros((NOCC, 32), BF16)], axis=1)
    pl.semaphore_wait(barrier, 12)

    sends = []

    def start(copy):
        copy.start()
        sends.append(copy)
        return copy

    steps = [
        start(push(zbuf.at[z], zbuf.at[z], gz_s.at[d - 1], gz_r.at[d - 1], pair, (z + d) % 4))
        for d in range(1, 4)
    ]
    for copy in steps:
        copy.wait_recv()
    whole = jnp.concatenate([zbuf[i][:, :96] for i in range(4)], axis=1)
    for k in range(3):
        gat[x, y, c, k] = whole[:, k * BS : (k + 1) * BS]
    spans = (pl.ds(0, 32), pl.ds(32, 32))

    def block(half, f, s):
        bx, by = ((x - f + 4) % 4, (y - s + 4) % 4) if half == 0 else ((x - s + 4) % 4, (y - f + 4) % 4)
        return gat.at[bx, by, c, :, spans[half]]

    def along(axis, d):
        return pair_of((x + d) % 4, y, c) if axis == 0 else pair_of(x, (y + d) % 4, c)

    def second(half, f):
        view = block(half, f, 0)
        for d in range(1, 4):
            start(push(view, view, gs_s.at[half, f, d - 1], gs_r.at[half, f, d - 1], along(1 - half, d), z))
        start(push(view, view, gc_s.at[half, f, 0], gc_r.at[half, f, 0], other, z))

    for d in (1, 3, 2):
        for half in range(2):
            view = block(half, 0, 0)
            start(push(view, view, ga_s.at[half, d - 1], ga_r.at[half, d - 1], along(half, d), z))
    for half in range(2):
        second(half, 0)
    for f in (1, 3, 2):
        for half in range(2):
            view = block(half, f, 0)
            push(view, view, ga_s.at[half, f - 1], ga_r.at[half, f - 1], other, z).wait_recv()
            second(half, f)
    for f in (0, 1, 3, 2):
        for d in (1, 3, 2):
            for half in range(2):
                view = block(half, f, d)
                push(view, view, gs_s.at[half, f, d - 1], gs_r.at[half, f, d - 1], other, z).wait_recv()
                start(push(view, view, gc_s.at[half, f, d], gc_r.at[half, f, d], other, z))
    for half in range(2):
        for f in range(4):
            for d in range(4):
                bx, by = ((x - f + 4) % 4, (y - d + 4) % 4) if half == 0 else ((x - d + 4) % 4, (y - f + 4) % 4)
                view = gat.at[bx, by, 1 - c, :, spans[half]]
                push(view, view, gc_s.at[half, f, d], gc_r.at[half, f, d], other, z).wait_recv()
    for copy in locals_:
        copy.wait()
    b_own.wait()
    start(push(b2.at[own_k], b2.at[own_k], b_sem.at[1], b_sem.at[2], other, z))

    for t in range(SLOTS):
        lam = ints[0, t]
        picked = gat[lam // 24, (lam // 6) % 4, (lam // 3) % 2, lam % 3]
        for s in range(SIG):
            keep = jnp.logical_and(ints[1, t] == s, ints[3, t] > 0)
            lhs[s * NOCC : (s + 1) * NOCC, t * BS : (t + 1) * BS] = jnp.where(
                keep, picked, jnp.zeros_like(picked)
            )

    @pl.loop(0, ROWS // 2, unroll=4)
    def _(q):
        parts = []
        for t in range(SLOTS):
            both = []
            for i in range(2):
                tile = tiles[t, 2 * q + i]
                both.append(jnp.where(2 * q + i < ints[2, t], tile, jnp.zeros_like(tile)))
            parts.append(jnp.concatenate(both, axis=1))
        got = jnp.dot(lhs[...], jnp.concatenate(parts, axis=0), preferred_element_type=F32)
        for i in range(2):
            for s in range(SIG):
                acc[s, pl.ds(2 * q + i, NOCC, stride=ROWS), :] = got[
                    s * NOCC : (s + 1) * NOCC, i * BS : (i + 1) * BS
                ]

    def z_load(k):
        for i in range(2):
            to = 0
            for (dx, dy), lo, hi in CHUNKS[k][i]:
                for core in range(2):
                    at = pl.multiple_of(pair_of((x + dx) % 4, (y + dy) % 4, core) * BR + lo, 16)
                    for s in range(SIG):
                        a[k, 2 * i + core, to : to + hi - lo, s * BS : (s + 1) * BS] = acc[
                            s, pl.ds(at, hi - lo), :
                        ].astype(BF16)
                to += hi - lo

    def cut(k, d):
        return (0, 48 - 16 * (k % 2)) if d == 1 else (48 - 16 * (k % 2), BR)

    def far_copy(k, d):
        lo, hi = cut(k, d)
        i = 0 if d == 1 else 1
        span = pl.ds(lo, hi - lo)
        return push(
            a.at[k, (z + 2) % 4, span], zra.at[k, span], za_s.at[k, i], za_r.at[k, i], pair, (z + d) % 4
        )

    def near_copy(k, d):
        i = 0 if d == 1 else 1
        return push(a.at[k, (z + d) % 4], zrb.at[k, i], zb_s.at[k, i], zb_r.at[k, i], pair, (z + d) % 4)

    def direct_copy(k, d):
        return push(
            a.at[k, (z + d) % 4], zdx.at[k, d - 1], ze_s.at[k, d - 1], ze_r.at[k, d - 1], pair, (z + d) % 4
        )

    def z_far(k):
        z_load(k)
        if k < DIRECT:
            for d in (1, 3, 2):
                start(direct_copy(k, d))
            return
        for d in (1, -1):
            start(far_copy(k, d))

    def z_near(k):
        if k < DIRECT:
            return
        for d in (1, -1):
            far_copy(k, d).wait_recv()
            unit = (z + d) % 4
            for r in range(*cut(k, d), 16):
                a[k, unit, r : r + 16] = (
                    a[k, unit, r : r + 16].astype(F32) + zra[k, r : r + 16].astype(F32)
                ).astype(BF16)
            start(near_copy(k, d))

    mine = z % 2 == c

    def out_copy(k, i):
        target, zt = (other, z) if i == 0 else (jnp.where(mine, pair, other), (z + (0, 1, 3, 2)[i]) % 4)
        return push(red.at[k], a2.at[k, c, z // 2], zc_s.at[k, i], zc_r.at[k, c, i], target, zt)

    def z_sum(k):
        if k < DIRECT:
            terms = [zdx.at[k, i] for i in range(3)]
            for d in (1, 3, 2):
                direct_copy(k, d).wait_recv()
        else:
            terms = [zrb.at[k, i] for i in range(2)]
            for d in (1, -1):
                near_copy(k, d).wait_recv()
        for r in range(0, BR, 16):
            total = a[k, z, r : r + 16].astype(F32)
            for term in terms:
                total = total + term[r : r + 16].astype(F32)
            red[k, r : r + 16] = total.astype(BF16)
        start(out_copy(k, 1))
        start(out_copy(k, 2))
        if k < DIRECT:
            start(out_copy(k, 3))

        @pl.when(mine)
        def _():
            a2[k, c, z // 2] = red[k]

        @pl.when(jnp.logical_not(mine))
        def _():
            out_copy(k, 0).start()

    def landed(k, core, zf, i):
        view = a2.at[k, core, zf // 2]
        return push(view, view, zc_s.at[k, i], zc_r.at[k, core, i], other, z)

    def on_copy(k, core):
        zf, zt = (down, up) if core == 0 else (up, down)
        view = a2.at[k, core, zf // 2]
        return push(view, view, zd_s.at[k, core], zd_r.at[k, core], pair, zt)

    def z_on(k):
        if k < DIRECT:
            return

        @pl.when(jnp.logical_not(mine))
        def _():
            for core, zf, i in ((0, down, 1), (1, up, 2)):
                landed(k, core, zf, i).wait_recv()
                on_copy(k, core).start()

    def z_end(k):
        @pl.when(mine)
        def _():
            landed(k, 1 - c, z, 0).wait_recv()
            for core in range(2):
                if k < DIRECT:
                    landed(k, core, (z + 2) % 4, 3).wait_recv()
                else:
                    view = a2.at[k, core, ((z + 2) % 4) // 2]
                    push(view, view, zd_s.at[k, core], zd_r.at[k, core], other, z).wait_recv()

        @pl.when(jnp.logical_not(mine))
        def _():
            landed(k, 1, down, 1).wait_recv()
            landed(k, 0, up, 2).wait_recv()
            if k < DIRECT:
                landed(k, 0, down, 1).wait_recv()
                landed(k, 1, up, 2).wait_recv()

    def multiply(k):
        left = jnp.concatenate([a2[k, i].reshape(2 * BR, KW) for i in range(2)], axis=1)
        for h in range(2):
            for at in range(0, HW, 512):
                width = min(512, HW - at)
                got = jnp.dot(
                    left, b2[:, h * HW + at : h * HW + at + width], preferred_element_type=F32
                )
                cc[k, h, :, :, at : at + width] = got.astype(BF16).reshape(2, BR, width)

    def held(h, f, s, p=0):
        k, i, at, lo, hi = PIECES[(f, s) if h == 0 else (s, f)][p]
        return cc.at[k, h, i, pl.ds(at, hi - lo)], lo, hi

    def add(into, terms, lo=0, hi=HW, out=None):
        for r in range(0, into.shape[0], 16):
            total = into[r : r + 16, lo:hi].astype(F32)
            for term in terms:
                total = total + term[r : r + 16, lo:hi].astype(F32)
            if out is None:
                into[r : r + 16, lo:hi] = total.astype(BF16)
            else:
                out_ref[r : r + 16, out : out + hi - lo] = total.astype(BF16)

    def columns(d):
        return pl.ds(0, CUT) if d == 1 else pl.ds(CUT, HW - CUT)

    def far(src, dst, send_sem, recv_sem, to):
        for i, d in enumerate((1, -1)):
            start(push(src.at[:, columns(d)], dst.at[:, columns(d)], send_sem.at[i], recv_sem.at[i], to[d], z))

    def near(block, p, d, far_dst, far_s, far_r, dst, send_sem, recv_sem, to):
        i = 0 if d == 1 else 1
        ref, lo, hi = block
        if p == 0:
            view = far_dst.at[:, columns(d)]
            push(view, view, far_s.at[i], far_r.at[i], to[d], z).wait_recv()
        span = pl.ds(lo, hi - lo)
        add(ref, [far_dst.at[span]], 0 if d == 1 else CUT, CUT if d == 1 else HW)
        start(push(ref, dst.at[i, span], send_sem.at[i, p], recv_sem.at[i, p], to[d], z))

    def arrived(dst, send_sem, recv_sem, blocks):
        for i in range(2):
            for p, (_, _, _, lo, hi) in enumerate(PIECES[blocks[i]]):
                view = dst.at[i, pl.ds(lo, hi - lo)]
                push(view, view, send_sem.at[i, p], recv_sem.at[i, p], other, z).wait_recv()

    def named(h, f, s):
        return (f, s) if h == 0 else (s, f)

    def far1(h, s):
        far(held(h, 2, s)[0], r1.at[h, s], r1_s.at[h, s], r1_r.at[h, s], axes1[h])

    def near1(h, s, d, p=0):
        near(
            held(h, d % 4, s, p), p, d, r1.at[h, s], r1_s.at[h, s], r1_r.at[h, s],
            r2.at[h, s], r2_s.at[h, s], r2_r.at[h, s], axes1[h],
        )

    def home1(h, s, p=0):
        if p == 0:
            arrived(r2.at[h, s], r2_s.at[h, s], r2_r.at[h, s], [named(h, 1, s), named(h, 3, s)])
        ref, lo, hi = held(h, 0, s, p)
        add(ref, [r2.at[h, s, i, pl.ds(lo, hi - lo)] for i in range(2)])

    def far2(h):
        far(held(h, 0, 2)[0], r3.at[h], r3_s.at[h], r3_r.at[h], axes2[h])

    def near2(h, d, p=0):
        near(
            held(h, 0, d % 4, p), p, d, r3.at[h], r3_s.at[h], r3_r.at[h],
            r4.at[h], r4_s.at[h], r4_r.at[h], axes2[h],
        )

    def final(h):
        arrived(r4.at[h], r4_s.at[h], r4_r.at[h], [named(h, 0, 1), named(h, 0, 3)])
        add(held(h, 0, 0)[0], [r4.at[h, 0], r4.at[h, 1]], out=h * HW)

    def b_wait():
        push(b2.at[other_k], b2.at[other_k], b_sem.at[1], b_sem.at[2], other, z).wait_recv()

    def first_multiply(k):
        if k == 0:
            b_wait()
        z_end(k)
        multiply(k)

    steps = {
        "zf": z_far, "zn": z_near, "zs": z_sum, "zo": z_on, "mm": first_multiply,
        "f1": far1, "n1": near1, "h1": home1, "f2": far2, "n2": near2, "fi": final,
    }
    for name, *where in ORDER:
        steps[name](*where)

    for copy in sends:
        copy.wait_send()
    for k in range(NC):

        @pl.when(jnp.logical_not(mine))
        def _():
            out_copy(k, 0).wait_send()
            if k >= DIRECT:
                for core in range(2):
                    on_copy(k, core).wait_send()


def fused(tiles, lam, sig, rows, mask, occ, b):
    sem = pltpu.SemaphoreType.DMA

    def vm(*shape):
        return pltpu.VMEM(shape, BF16)

    def twice(*shapes):
        return [sem(shape) for shape in shapes for _ in range(2)]

    hbm = pl.BlockSpec(memory_space=pl.ANY)
    vmem = pl.BlockSpec(memory_space=pltpu.VMEM)
    return pl.pallas_call(
        fused_kernel,
        out_shape=jax.ShapeDtypeStruct((BR, NW), BF16),
        in_specs=[hbm] * 7,
        out_specs=vmem,
        scratch_shapes=[
            vm(SLOTS, ROWS, BS, BS),
            pltpu.SMEM((4, SLOTS), jnp.int32),
            vm(2 * KW, NW),
            vm(NOCC, 96),
            vm(4, NOCC, BS),
            vm(4, 4, 2, 3, NOCC, BS),
            vm(SIG * NOCC, SLOTS * BS),
            pltpu.VMEM((SIG, NOCC * ROWS, BS), F32),
            vm(NC, 4, BR, KW),
            vm(NC, BR, KW),
            vm(NC, 2, BR, KW),
            vm(max(DIRECT, 1), 3, BR, KW),
            vm(NC, BR, KW),
            vm(NC, 2, 2, BR, KW),
            vm(NC, 2, 2, BR, HW),
            vm(2, 4, BR, HW),
            vm(2, 4, 2, BR, HW),
            vm(2, BR, HW),
            vm(2, 2, BR, HW),
            sem((8,)),
            sem((4,)),
            *twice((3,), (2, 3), (2, 4, 3), (2, 4, 4)),
            *twice((NC, 2), (NC, 2), (max(DIRECT, 1), 3)),
            sem((NC, 4)),
            sem((NC, 2, 4)),
            *twice((NC, 2), (2, 4, 2), (2, 4, 2, 2), (2, 2), (2, 2, 2)),
        ],
        compiler_params=pltpu.CompilerParams(
            collective_id=0, has_side_effects=True, vmem_limit_bytes=60 * 2**20
        ),
        name="fused",
    )(tiles, lam, sig, rows, mask, occ, b)


def body(integral_tiles, tile_lam, tile_sig, tile_rows, screen_mask, occ_panel, virt_panel):
    out = fused(
        integral_tiles, tile_lam, tile_sig, tile_rows, screen_mask, occ_panel, virt_panel
    )
    return out.reshape(2, ROWS, NW)


def solution(mesh):
    return jax.shard_map(
        body,
        mesh=mesh,
        in_specs=(
            P(("pair", "orb"), None, None, None),
            P(("pair", "orb")),
            P(("pair", "orb")),
            P(("pair", "orb")),
            P(("pair", "orb")),
            P(None, ("pair", "orb")),
            P("pair", "orb"),
        ),
        out_specs=P("pair", None, "orb"),
        check_vma=False,
    )
```

```python
import jax
import jax.numpy as jnp
from jax import lax
from jax.experimental import pallas as pl
from jax.experimental.pallas import tpu as pltpu
from jax.sharding import PartitionSpec as P

BS = 128
NOCC = 64
ROWS = 40
SLOTS = 12
NBLK = 96
SIG = 3
KW = 384
NW = 2816
HW = NW // 2
CUT = 768
BR = 80
MESH = pl.DeviceIdType.MESH
F32 = jnp.float32
BF16 = jnp.bfloat16

CHUNKS = [
    [[((2, 1), 0, BR)], [((1, 2), 0, BR)]],
    [[((2, 3), 0, BR)], [((3, 2), 0, BR)]],
    [[((1, 1), 0, 48), ((3, 3), 0, 32)], [((2, 2), 0, BR)]],
    [[((1, 3), 0, BR)], [((3, 1), 0, BR)]],
    [[((0, 3), 0, 32), ((3, 0), 0, 48)], [((2, 0), 0, BR)]],
    [[((1, 1), 48, BR), ((3, 3), 32, BR)], [((0, 2), 0, BR)]],
    [[((0, 1), 0, BR)], [((1, 0), 0, BR)]],
    [[((0, 3), 32, BR), ((3, 0), 48, BR)], [((0, 0), 0, BR)]],
]
NC = len(CHUNKS)
DIRECT = 3

ORDER = [
    ("zf", 0), ("zf", 1), ("zf", 2), ("zs", 0), ("zf", 3), ("zs", 1), ("zf", 4), ("zs", 2), ("zf", 5), ("mm", 0),
    ("f1", 0, 1), ("f1", 1, 1), ("zn", 3), ("mm", 1), ("f1", 0, 3), ("f1", 1, 3), ("zn", 4), ("mm", 2),
    ("f1", 0, 2), ("f1", 1, 2), ("zn", 5), ("n1", 0, 1, 1, 0), ("n1", 1, 1, 1, 0), ("zs", 3), ("n1", 0, 3, -1, 0),
    ("n1", 1, 3, -1, 0), ("zs", 4), ("zs", 5), ("n1", 0, 2, -1, 0), ("n1", 1, 2, -1, 0), ("n1", 0, 2, 1, 0),
    ("n1", 1, 2, 1, 0), ("zo", 3), ("zf", 6), ("zo", 4), ("zf", 7), ("zo", 5), ("mm", 3), ("zn", 6),
    ("n1", 0, 1, -1, 0), ("n1", 0, 3, 1, 0), ("n1", 1, 1, -1, 0), ("zn", 7), ("n1", 1, 3, 1, 0), ("mm", 4),
    ("f1", 0, 0), ("mm", 5), ("f1", 1, 0), ("zs", 6), ("n1", 0, 1, 1, 1), ("n1", 0, 3, -1, 1), ("n1", 1, 1, 1, 1),
    ("zs", 7), ("n1", 1, 3, -1, 1), ("h1", 0, 2, 0), ("f2", 0), ("h1", 1, 2, 0), ("f2", 1), ("zo", 6), ("zo", 7),
    ("n1", 0, 0, -1, 0), ("n1", 1, 0, -1, 0), ("mm", 6), ("n1", 0, 0, 1, 0), ("n1", 1, 0, 1, 0), ("mm", 7),
    ("n1", 0, 0, -1, 1), ("n1", 1, 0, -1, 1), ("h1", 0, 1, 0), ("h1", 0, 3, 0), ("h1", 0, 3, 1), ("h1", 1, 1, 0),
    ("h1", 1, 3, 0), ("h1", 1, 3, 1), ("n2", 1, -1, 0), ("n2", 1, -1, 1), ("n2", 0, -1, 0), ("n2", 0, -1, 1),
    ("n2", 1, 1, 0), ("n2", 0, 1, 0), ("h1", 0, 0, 0), ("h1", 1, 0, 0), ("fi", 1), ("fi", 0),
]


def pieces():
    found = {}
    for k, chunk in enumerate(CHUNKS):
        for i, parts in enumerate(chunk):
            at = 0
            for block, lo, hi in parts:
                found.setdefault(block, []).append((k, i, at, lo, hi))
                at += hi - lo
    return found


PIECES = pieces()


def pair_of(x, y, c):
    return (x * 4 + y) * 2 + c


def push(src, dst, send_sem, recv_sem, pair, z):
    return pltpu.make_async_remote_copy(
        src_ref=src,
        dst_ref=dst,
        send_sem=send_sem,
        recv_sem=recv_sem,
        device_id=(pair, z),
        device_id_type=MESH,
    )


def fused_kernel(
    tiles_hbm, lam_hbm, sig_hbm, rows_hbm, mask_hbm, occ_hbm, b_hbm, out_ref,
    tiles, ints, b2, panel, zbuf, gat, lhs, acc, a, zra, zrb, zdx, red, a2, cc, r1, r2, r3, r4,
    in_sem, b_sem, gz_s, gz_r, ga_s, ga_r, gs_s, gs_r, gc_s, gc_r,
    za_s, za_r, zb_s, zb_r, ze_s, ze_r, zc_s, zc_r, zd_s, zd_r,
    r1_s, r1_r, r2_s, r2_r, r3_s, r3_r, r4_s, r4_r,
):
    pair = lax.axis_index("pair")
    z = lax.axis_index("orb")
    x, y, c = pair // 8, (pair // 2) % 4, pair % 2
    other = pair_of(x, y, 1 - c)
    up, down = (z + 1) % 4, (z + 3) % 4
    xs = {1: pair_of((x + 1) % 4, y, c), -1: pair_of((x + 3) % 4, y, c)}
    ys = {1: pair_of(x, (y + 1) % 4, c), -1: pair_of(x, (y + 3) % 4, c)}
    axes1, axes2 = (xs, ys), (ys, xs)

    own_k = pl.ds(pl.multiple_of(c * KW, BS), KW)
    other_k = pl.ds(pl.multiple_of((1 - c) * KW, BS), KW)
    occ_own = pltpu.make_async_copy(occ_hbm, panel, b_sem.at[3])
    occ_own.start()
    b_own = pltpu.make_async_copy(b_hbm, b2.at[own_k], b_sem.at[0])
    locals_ = []
    for i, ref in enumerate((lam_hbm, sig_hbm, rows_hbm, mask_hbm)):
        locals_.append(pltpu.make_async_copy(ref, ints.at[i], in_sem.at[i]))
    for i in range(4):
        part = pl.ds(3 * i, 3)
        locals_.append(pltpu.make_async_copy(tiles_hbm.at[part], tiles.at[part], in_sem.at[4 + i]))
    for copy in locals_:
        copy.start()
    b_own.start()

    barrier = pltpu.get_barrier_semaphore()

    def hello(pair_id, z_id):
        pl.semaphore_signal(barrier, inc=1, device_id=(pair_id, z_id), device_id_type=MESH)

    hello(other, z)
    hello(other, up)
    hello(other, down)
    for d in range(1, 4):
        hello(pair_of((x + d) % 4, y, c), z)
        hello(pair_of(x, (y + d) % 4, c), z)
        hello(pair, (z + d) % 4)
    occ_own.wait()
    zbuf[z] = jnp.concatenate([panel[...], jnp.zeros((NOCC, 32), BF16)], axis=1)
    pl.semaphore_wait(barrier, 12)

    sends = []

    def start(copy):
        copy.start()
        sends.append(copy)
        return copy

    steps = [
        start(push(zbuf.at[z], zbuf.at[z], gz_s.at[d - 1], gz_r.at[d - 1], pair, (z + d) % 4))
        for d in range(1, 4)
    ]
    for copy in steps:
        copy.wait_recv()
    whole = jnp.concatenate([zbuf[i][:, :96] for i in range(4)], axis=1)
    for k in range(3):
        gat[x, y, c, k] = whole[:, k * BS : (k + 1) * BS]
    spans = (pl.ds(0, 32), pl.ds(32, 32))

    def block(half, f, s):
        bx, by = ((x - f + 4) % 4, (y - s + 4) % 4) if half == 0 else ((x - s + 4) % 4, (y - f + 4) % 4)
        return gat.at[bx, by, c, :, spans[half]]

    def along(axis, d):
        return pair_of((x + d) % 4, y, c) if axis == 0 else pair_of(x, (y + d) % 4, c)

    def second(half, f):
        view = block(half, f, 0)
        for d in range(1, 4):
            start(push(view, view, gs_s.at[half, f, d - 1], gs_r.at[half, f, d - 1], along(1 - half, d), z))
        start(push(view, view, gc_s.at[half, f, 0], gc_r.at[half, f, 0], other, z))

    for d in (1, 3, 2):
        for half in range(2):
            view = block(half, 0, 0)
            start(push(view, view, ga_s.at[half, d - 1], ga_r.at[half, d - 1], along(half, d), z))
    for half in range(2):
        second(half, 0)
    for f in (1, 3, 2):
        for half in range(2):
            view = block(half, f, 0)
            push(view, view, ga_s.at[half, f - 1], ga_r.at[half, f - 1], other, z).wait_recv()
            second(half, f)
    for f in (0, 1, 3, 2):
        for d in (1, 3, 2):
            for half in range(2):
                view = block(half, f, d)
                push(view, view, gs_s.at[half, f, d - 1], gs_r.at[half, f, d - 1], other, z).wait_recv()
                start(push(view, view, gc_s.at[half, f, d], gc_r.at[half, f, d], other, z))
    for half in range(2):
        for f in range(4):
            for d in range(4):
                bx, by = ((x - f + 4) % 4, (y - d + 4) % 4) if half == 0 else ((x - d + 4) % 4, (y - f + 4) % 4)
                view = gat.at[bx, by, 1 - c, :, spans[half]]
                push(view, view, gc_s.at[half, f, d], gc_r.at[half, f, d], other, z).wait_recv()
    for copy in locals_:
        copy.wait()
    b_own.wait()
    start(push(b2.at[own_k], b2.at[own_k], b_sem.at[1], b_sem.at[2], other, z))

    for t in range(SLOTS):
        lam = ints[0, t]
        picked = gat[lam // 24, (lam // 6) % 4, (lam // 3) % 2, lam % 3]
        for s in range(SIG):
            keep = jnp.logical_and(ints[1, t] == s, ints[3, t] > 0)
            lhs[s * NOCC : (s + 1) * NOCC, t * BS : (t + 1) * BS] = jnp.where(
                keep, picked, jnp.zeros_like(picked)
            )

    @pl.loop(0, ROWS // 2, unroll=10)
    def _(q):
        parts = []
        for t in range(SLOTS):
            both = []
            for i in range(2):
                tile = tiles[t, 2 * q + i]
                both.append(jnp.where(2 * q + i < ints[2, t], tile, jnp.zeros_like(tile)))
            parts.append(jnp.concatenate(both, axis=1))
        got = jnp.dot(lhs[...], jnp.concatenate(parts, axis=0), preferred_element_type=F32)
        for i in range(2):
            for s in range(SIG):
                acc[s, pl.ds(2 * q + i, NOCC, stride=ROWS), :] = got[
                    s * NOCC : (s + 1) * NOCC, i * BS : (i + 1) * BS
                ]

    def z_load(k):
        for i in range(2):
            to = 0
            for (dx, dy), lo, hi in CHUNKS[k][i]:
                for core in range(2):
                    at = pl.multiple_of(pair_of((x + dx) % 4, (y + dy) % 4, core) * BR + lo, 16)
                    for s in range(SIG):
                        a[k, 2 * i + core, to : to + hi - lo, s * BS : (s + 1) * BS] = acc[
                            s, pl.ds(at, hi - lo), :
                        ].astype(BF16)
                to += hi - lo

    def cut(k, d):
        return (0, 48 - 16 * (k % 2)) if d == 1 else (48 - 16 * (k % 2), BR)

    def far_copy(k, d):
        lo, hi = cut(k, d)
        i = 0 if d == 1 else 1
        span = pl.ds(lo, hi - lo)
        return push(
            a.at[k, (z + 2) % 4, span], zra.at[k, span], za_s.at[k, i], za_r.at[k, i], pair, (z + d) % 4
        )

    def near_copy(k, d):
        i = 0 if d == 1 else 1
        return push(a.at[k, (z + d) % 4], zrb.at[k, i], zb_s.at[k, i], zb_r.at[k, i], pair, (z + d) % 4)

    def direct_copy(k, d):
        return push(
            a.at[k, (z + d) % 4], zdx.at[k, d - 1], ze_s.at[k, d - 1], ze_r.at[k, d - 1], pair, (z + d) % 4
        )

    def z_far(k):
        z_load(k)
        if k < DIRECT:
            for d in (1, 3, 2):
                start(direct_copy(k, d))
            return
        for d in (1, -1):
            start(far_copy(k, d))

    def z_near(k):
        if k < DIRECT:
            return
        for d in (1, -1):
            far_copy(k, d).wait_recv()
            unit = (z + d) % 4
            for r in range(*cut(k, d), 16):
                a[k, unit, r : r + 16] = (
                    a[k, unit, r : r + 16].astype(F32) + zra[k, r : r + 16].astype(F32)
                ).astype(BF16)
            start(near_copy(k, d))

    mine = z % 2 == c

    def out_copy(k, i):
        target, zt = (other, z) if i == 0 else (jnp.where(mine, pair, other), (z + (0, 1, 3, 2)[i]) % 4)
        return push(red.at[k], a2.at[k, c, z // 2], zc_s.at[k, i], zc_r.at[k, c, i], target, zt)

    def z_sum(k):
        if k < DIRECT:
            terms = [zdx.at[k, i] for i in range(3)]
            for d in (1, 3, 2):
                direct_copy(k, d).wait_recv()
        else:
            terms = [zrb.at[k, i] for i in range(2)]
            for d in (1, -1):
                near_copy(k, d).wait_recv()
        for r in range(0, BR, 16):
            total = a[k, z, r : r + 16].astype(F32)
            for term in terms:
                total = total + term[r : r + 16].astype(F32)
            red[k, r : r + 16] = total.astype(BF16)
        start(out_copy(k, 1))
        start(out_copy(k, 2))
        if k < DIRECT:
            start(out_copy(k, 3))

        @pl.when(mine)
        def _():
            a2[k, c, z // 2] = red[k]

        @pl.when(jnp.logical_not(mine))
        def _():
            out_copy(k, 0).start()

    def landed(k, core, zf, i):
        view = a2.at[k, core, zf // 2]
        return push(view, view, zc_s.at[k, i], zc_r.at[k, core, i], other, z)

    def on_copy(k, core):
        zf, zt = (down, up) if core == 0 else (up, down)
        view = a2.at[k, core, zf // 2]
        return push(view, view, zd_s.at[k, core], zd_r.at[k, core], pair, zt)

    def z_on(k):
        if k < DIRECT:
            return

        @pl.when(jnp.logical_not(mine))
        def _():
            for core, zf, i in ((0, down, 1), (1, up, 2)):
                landed(k, core, zf, i).wait_recv()
                on_copy(k, core).start()

    def z_end(k):
        @pl.when(mine)
        def _():
            landed(k, 1 - c, z, 0).wait_recv()
            for core in range(2):
                if k < DIRECT:
                    landed(k, core, (z + 2) % 4, 3).wait_recv()
                else:
                    view = a2.at[k, core, ((z + 2) % 4) // 2]
                    push(view, view, zd_s.at[k, core], zd_r.at[k, core], other, z).wait_recv()

        @pl.when(jnp.logical_not(mine))
        def _():
            landed(k, 1, down, 1).wait_recv()
            landed(k, 0, up, 2).wait_recv()
            if k < DIRECT:
                landed(k, 0, down, 1).wait_recv()
                landed(k, 1, up, 2).wait_recv()

    def multiply(k):
        left = jnp.concatenate([a2[k, i].reshape(2 * BR, KW) for i in range(2)], axis=1)
        for h in range(2):
            for at in range(0, HW, 512):
                width = min(512, HW - at)
                got = jnp.dot(
                    left, b2[:, h * HW + at : h * HW + at + width], preferred_element_type=F32
                )
                cc[k, h, :, :, at : at + width] = got.astype(BF16).reshape(2, BR, width)

    def held(h, f, s, p=0):
        k, i, at, lo, hi = PIECES[(f, s) if h == 0 else (s, f)][p]
        return cc.at[k, h, i, pl.ds(at, hi - lo)], lo, hi

    def add(into, terms, lo=0, hi=HW, out=None):
        for r in range(0, into.shape[0], 16):
            total = into[r : r + 16, lo:hi].astype(F32)
            for term in terms:
                total = total + term[r : r + 16, lo:hi].astype(F32)
            if out is None:
                into[r : r + 16, lo:hi] = total.astype(BF16)
            else:
                out_ref[r : r + 16, out : out + hi - lo] = total.astype(BF16)

    def columns(d):
        return pl.ds(0, CUT) if d == 1 else pl.ds(CUT, HW - CUT)

    def far(src, dst, send_sem, recv_sem, to):
        for i, d in enumerate((1, -1)):
            start(push(src.at[:, columns(d)], dst.at[:, columns(d)], send_sem.at[i], recv_sem.at[i], to[d], z))

    def near(block, p, d, far_dst, far_s, far_r, dst, send_sem, recv_sem, to):
        i = 0 if d == 1 else 1
        ref, lo, hi = block
        if p == 0:
            view = far_dst.at[:, columns(d)]
            push(view, view, far_s.at[i], far_r.at[i], to[d], z).wait_recv()
        span = pl.ds(lo, hi - lo)
        add(ref, [far_dst.at[span]], 0 if d == 1 else CUT, CUT if d == 1 else HW)
        start(push(ref, dst.at[i, span], send_sem.at[i, p], recv_sem.at[i, p], to[d], z))

    def arrived(dst, send_sem, recv_sem, blocks):
        for i in range(2):
            for p, (_, _, _, lo, hi) in enumerate(PIECES[blocks[i]]):
                view = dst.at[i, pl.ds(lo, hi - lo)]
                push(view, view, send_sem.at[i, p], recv_sem.at[i, p], other, z).wait_recv()

    def named(h, f, s):
        return (f, s) if h == 0 else (s, f)

    def far1(h, s):
        far(held(h, 2, s)[0], r1.at[h, s], r1_s.at[h, s], r1_r.at[h, s], axes1[h])

    def near1(h, s, d, p=0):
        near(
            held(h, d % 4, s, p), p, d, r1.at[h, s], r1_s.at[h, s], r1_r.at[h, s],
            r2.at[h, s], r2_s.at[h, s], r2_r.at[h, s], axes1[h],
        )

    def home1(h, s, p=0):
        if p == 0:
            arrived(r2.at[h, s], r2_s.at[h, s], r2_r.at[h, s], [named(h, 1, s), named(h, 3, s)])
        ref, lo, hi = held(h, 0, s, p)
        add(ref, [r2.at[h, s, i, pl.ds(lo, hi - lo)] for i in range(2)])

    def far2(h):
        far(held(h, 0, 2)[0], r3.at[h], r3_s.at[h], r3_r.at[h], axes2[h])

    def near2(h, d, p=0):
        near(
            held(h, 0, d % 4, p), p, d, r3.at[h], r3_s.at[h], r3_r.at[h],
            r4.at[h], r4_s.at[h], r4_r.at[h], axes2[h],
        )

    def final(h):
        arrived(r4.at[h], r4_s.at[h], r4_r.at[h], [named(h, 0, 1), named(h, 0, 3)])
        add(held(h, 0, 0)[0], [r4.at[h, 0], r4.at[h, 1]], out=h * HW)

    def b_wait():
        push(b2.at[other_k], b2.at[other_k], b_sem.at[1], b_sem.at[2], other, z).wait_recv()

    def first_multiply(k):
        if k == 0:
            b_wait()
        z_end(k)
        multiply(k)

    steps = {
        "zf": z_far, "zn": z_near, "zs": z_sum, "zo": z_on, "mm": first_multiply,
        "f1": far1, "n1": near1, "h1": home1, "f2": far2, "n2": near2, "fi": final,
    }
    def drain():
        for copy in sends:
            copy.wait_send()
        for k in range(NC):

            @pl.when(jnp.logical_not(mine))
            def _():
                out_copy(k, 0).wait_send()
                if k >= DIRECT:
                    for core in range(2):
                        on_copy(k, core).wait_send()

    for name, *where in ORDER:
        if name == "fi" and sends:
            drain()
            sends.clear()
        steps[name](*where)


def fused(tiles, lam, sig, rows, mask, occ, b):
    sem = pltpu.SemaphoreType.DMA

    def vm(*shape):
        return pltpu.VMEM(shape, BF16)

    def twice(*shapes):
        return [sem(shape) for shape in shapes for _ in range(2)]

    hbm = pl.BlockSpec(memory_space=pl.ANY)
    vmem = pl.BlockSpec(memory_space=pltpu.VMEM)
    return pl.pallas_call(
        fused_kernel,
        out_shape=jax.ShapeDtypeStruct((BR, NW), BF16),
        in_specs=[hbm] * 7,
        out_specs=vmem,
        scratch_shapes=[
            vm(SLOTS, ROWS, BS, BS),
            pltpu.SMEM((4, SLOTS), jnp.int32),
            vm(2 * KW, NW),
            vm(NOCC, 96),
            vm(4, NOCC, BS),
            vm(4, 4, 2, 3, NOCC, BS),
            vm(SIG * NOCC, SLOTS * BS),
            pltpu.VMEM((SIG, NOCC * ROWS, BS), F32),
            vm(NC, 4, BR, KW),
            vm(NC, BR, KW),
            vm(NC, 2, BR, KW),
            vm(max(DIRECT, 1), 3, BR, KW),
            vm(NC, BR, KW),
            vm(NC, 2, 2, BR, KW),
            vm(NC, 2, 2, BR, HW),
            vm(2, 4, BR, HW),
            vm(2, 4, 2, BR, HW),
            vm(2, BR, HW),
            vm(2, 2, BR, HW),
            sem((8,)),
            sem((4,)),
            *twice((3,), (2, 3), (2, 4, 3), (2, 4, 4)),
            *twice((NC, 2), (NC, 2), (max(DIRECT, 1), 3)),
            sem((NC, 4)),
            sem((NC, 2, 4)),
            *twice((NC, 2), (2, 4, 2), (2, 4, 2, 2), (2, 2), (2, 2, 2)),
        ],
        compiler_params=pltpu.CompilerParams(
            collective_id=0, has_side_effects=True, vmem_limit_bytes=60 * 2**20
        ),
        name="fused",
    )(tiles, lam, sig, rows, mask, occ, b)


def body(integral_tiles, tile_lam, tile_sig, tile_rows, screen_mask, occ_panel, virt_panel):
    out = fused(
        integral_tiles, tile_lam, tile_sig, tile_rows, screen_mask, occ_panel, virt_panel
    )
    return out.reshape(2, ROWS, NW)


def solution(mesh):
    return jax.shard_map(
        body,
        mesh=mesh,
        in_specs=(
            P(("pair", "orb"), None, None, None),
            P(("pair", "orb")),
            P(("pair", "orb")),
            P(("pair", "orb")),
            P(("pair", "orb")),
            P(None, ("pair", "orb")),
            P("pair", "orb"),
        ),
        out_specs=P("pair", None, "orb"),
        check_vma=False,
    )
```
